512 devices in a mesh: video: 64 (over x, y, core), audio: 8 (over z).
Axes of the slice: x: 4, y: 8, z: 8, core: 2. Of those that a mesh axis runs over, the one named last changes fastest.
Arguments:
- video_query: bfloat16 [65536, 3072], P('video', 'audio'), may hold values from -12 to 12
- video_key: bfloat16 [65536, 3072], P('video', 'audio'), may hold values from -12 to 12
- video_value: bfloat16 [65536, 3072], P('video', 'audio'), may hold values from -6 to 6
- audio_query: bfloat16 [8192, 3072], P('video', 'audio'), may hold values from -12 to 12
- audio_key: bfloat16 [8192, 3072], P('video', 'audio'), may hold values from -12 to 12
- audio_value: bfloat16 [8192, 3072], P('video', 'audio'), may hold values from -6 to 6
- video_query_gain: float32 [3072], P('audio'), may hold values from 0.5 to 2
- video_key_gain: float32 [3072], P('audio'), may hold values from 0.5 to 2
- audio_query_gain: float32 [3072], P('audio'), may hold values from 0.5 to 2
- audio_key_gain: float32 [3072], P('audio'), may hold values from 0.5 to 2
- block_pairs: int32 [64, 16], replicated, may hold values from 0 to 511, as said below
Outputs:
- video_mixed: float32 [65536, 3072], P('video', 'audio')
- audio_mixed: float32 [8192, 3072], P('video', 'audio')
The draws below stay inside these ranges and needn't reach their ends.
Inputs may be any that keep to these rules, and one draw needn't show every extreme that they name: `block_pairs`: each row holds 16 different video blocks; a block v named in row a satisfies |(v * 128) // 1024 - (a * 128) // 128| <= 2; every video block is named in some row.
All inputs are finite; a program needn't handle non-finite values.
Results may differ from the reference program's by a relative error of at most 0.011.
Values may be sent and summed in bfloat16 or wider, within the bound.
A program may use at most 64 MiB of HBM per device.

```python
import math
import jax
import jax.numpy as jnp
from jax import lax

H = 24
E = 128
BLOCK = 128
TV_DEV = 1024
TA_DEV = 128
PAIRS = 16
REACH = 2
NV = 65536
NA = 8192
N_VIDEO = 64


def head_scales(base):
    heads = (jnp.arange(H * E) // E).astype(jnp.float32)
    return base ** (heads / max(H - 1, 1))


def rough_rows(key, count):
    drawn = jnp.clip(jax.random.normal(key, (count, H * E), jnp.float32), -6.0, 6.0)
    return (drawn * head_scales(math.sqrt(3.0))[None, :]).astype(jnp.bfloat16)


def draw_video_query(key, part):
    key = jax.random.fold_in(key, 11)
    return rough_rows(key, NV)


def draw_video_key(key, part):
    key = jax.random.fold_in(key, 12)
    return rough_rows(key, NV)


def draw_audio_query(key, part):
    key = jax.random.fold_in(key, 13)
    return rough_rows(key, NA)


def draw_audio_key(key, part):
    key = jax.random.fold_in(key, 14)
    return rough_rows(key, NA)


def draw_block_pairs(key, part):
    key = jax.random.fold_in(key, 5)
    audio_count = NA // BLOCK
    video_count = NV // BLOCK
    video_span = TV_DEV // BLOCK
    audio_span = TA_DEV // BLOCK
    per_audio = video_span // audio_span
    window = (2 * REACH + 1) * video_span
    rows = jnp.arange(audio_count, dtype=jnp.int32)
    first = (rows // audio_span - REACH) * video_span
    offsets = jnp.arange(window, dtype=jnp.int32)
    candidates = first[:, None] + offsets[None, :]
    aligned_low = rows * per_audio
    usable = (candidates >= 0) & (candidates < video_count)
    usable = usable & ((candidates < aligned_low[:, None]) | (candidates >= aligned_low[:, None] + per_audio))
    noise = jax.random.randint(key, (audio_count, window), 0, 1 << 20)
    ranking = jnp.where(usable, noise * window + offsets[None, :], -1 - offsets[None, :])
    chosen_scores, chosen = lax.top_k(ranking, PAIRS - per_audio)
    extra = jnp.take_along_axis(candidates, chosen, axis=1)
    aligned = aligned_low[:, None] + jnp.arange(per_audio, dtype=jnp.int32)[None, :]
    return jnp.concatenate([aligned, extra], axis=1).astype(jnp.int32)


def level_of(stream_key, shape, cuts, low, largest):
    loudness, own = 1.0, jax.random.fold_in(stream_key, 6)
    for axis_at, parts in cuts:
        draws = jnp.exp(jax.random.uniform(jax.random.fold_in(own, axis_at), (parts,), jnp.float32, low / len(cuts), largest / len(cuts)))
        loudness = loudness * jnp.repeat(draws, shape[axis_at] // parts).reshape([-1 if axis == axis_at else 1 for axis in range(len(shape))])
    return loudness


def bell_draw(own_key, extent, spread, bound, cuts=(), kind=jnp.bfloat16):
    drawn = spread * jax.random.normal(own_key, extent, jnp.float32)
    if cuts:
        drawn = drawn * level_of(own_key, extent, cuts, -0.22, 0.18)
    return jnp.clip(drawn, -bound, bound).astype(kind)


def setup_inputs(seed: int = 0) -> dict:
    arg_keys = jax.random.split(jax.random.key(seed), 12)
    video_query = draw_video_query(jax.random.fold_in(arg_keys[11], 71), 0)
    video_key = draw_video_key(jax.random.fold_in(arg_keys[11], 71), 0)
    video_value = bell_draw(arg_keys[2], (NV, H * E), 1.0, 6.0, ((0, 64), (1, 8)))
    audio_query = draw_audio_query(jax.random.fold_in(arg_keys[11], 71), 0)
    audio_key = draw_audio_key(jax.random.fold_in(arg_keys[11], 71), 0)
    audio_value = bell_draw(arg_keys[5], (NA, H * E), 1.0, 6.0, ((0, 64), (1, 8)))
    video_query_gain = jnp.clip(jnp.exp(math.log(2.0) - 1.3862944 * jax.random.uniform(arg_keys[6], (H * E,), jnp.float32) ** level_of(arg_keys[6], (H * E,), ((0, 8),), -0.2, 0.2)), 0.5, 2.0)
    video_key_gain = jnp.clip(jnp.exp(math.log(2.0) - 1.3862944 * jax.random.uniform(arg_keys[7], (H * E,), jnp.float32) ** level_of(arg_keys[7], (H * E,), ((0, 8),), -0.2, 0.2)), 0.5, 2.0)
    audio_query_gain = jnp.clip(jnp.exp(math.log(2.0) - 1.3862944 * jax.random.uniform(arg_keys[8], (H * E,), jnp.float32) ** level_of(arg_keys[8], (H * E,), ((0, 8),), -0.2, 0.2)), 0.5, 2.0)
    audio_key_gain = jnp.clip(jnp.exp(math.log(2.0) - 1.3862944 * jax.random.uniform(arg_keys[9], (H * E,), jnp.float32) ** level_of(arg_keys[9], (H * E,), ((0, 8),), -0.2, 0.2)), 0.5, 2.0)
    block_pairs = draw_block_pairs(jax.random.fold_in(arg_keys[11], 71), 0)
    return {"video_query": video_query, "video_key": video_key, "video_value": video_value, "audio_query": audio_query, "audio_key": audio_key, "audio_value": audio_value, "video_query_gain": video_query_gain, "video_key_gain": video_key_gain, "audio_query_gain": audio_query_gain, "audio_key_gain": audio_key_gain, "block_pairs": block_pairs}


EPS = 1e-06
MASKED = -1e+30

def block_mask(pairs, count):
    named = pairs[:, :, None] == jnp.arange(count, dtype=jnp.int32)[None, None, :]
    return jnp.any(named, axis=1)

def normalize(source, gain):
    wide = source.astype(jnp.float32)
    total = lax.optimization_barrier(jnp.sum(wide * wide, axis=1, keepdims=True))
    return (wide * lax.rsqrt(total / wide.shape[1] + EPS) * gain[None, :]).astype(jnp.bfloat16)

def attend(queries, key_rows, values, allowed):
    query_count = queries.shape[0]
    key_count = key_rows.shape[0]
    q_wide = queries.astype(jnp.float32).reshape(query_count, H, E)
    k_wide = key_rows.astype(jnp.float32).reshape(key_count, H, E)
    v_wide = values.astype(jnp.float32).reshape(key_count, H, E)
    scores = jnp.einsum('qhe,khe->hqk', q_wide, k_wide) * (1.0 / math.sqrt(E))
    shaped = scores.reshape(H, query_count // BLOCK, BLOCK, key_count // BLOCK, BLOCK)
    allowed_here = allowed[None, :, None, :, None]
    shaped = jnp.where(allowed_here, shaped, MASKED)
    row_max = lax.optimization_barrier(jnp.max(shaped, axis=(3, 4), keepdims=True))
    weights = jnp.where(allowed_here, jnp.exp(shaped - row_max), 0.0)
    row_total = lax.optimization_barrier(jnp.sum(weights, axis=(3, 4))).reshape(H, query_count)
    rounded = lax.optimization_barrier(weights.astype(jnp.bfloat16)).astype(jnp.float32)
    rounded = rounded.reshape(H, query_count, key_count)
    blended = jnp.einsum('hqk,khe->qhe', rounded, v_wide) / row_total.T[:, :, None]
    return blended.reshape(query_count, H * E).astype(jnp.float32)

def reference(video_query, video_key, video_value, audio_query, audio_key, audio_value, video_query_gain, video_key_gain, audio_query_gain, audio_key_gain, block_pairs):
    video_queries = normalize(video_query, video_query_gain)
    video_keys = normalize(video_key, video_key_gain)
    audio_queries = normalize(audio_query, audio_query_gain)
    audio_keys = normalize(audio_key, audio_key_gain)
    video_span = TV_DEV // BLOCK
    audio_span = TA_DEV // BLOCK
    window = 2 * REACH + 1
    pairs_mask = block_mask(block_pairs, NV // BLOCK)
    row_padded = jnp.pad(pairs_mask, ((REACH * audio_span, REACH * audio_span), (0, 0)))
    col_padded = jnp.pad(pairs_mask, ((0, 0), (REACH * video_span, REACH * video_span)))
    audio_keys_pad = jnp.pad(audio_keys, ((REACH * TA_DEV, REACH * TA_DEV), (0, 0)))
    audio_values_pad = jnp.pad(audio_value, ((REACH * TA_DEV, REACH * TA_DEV), (0, 0)))
    video_keys_pad = jnp.pad(video_keys, ((REACH * TV_DEV, REACH * TV_DEV), (0, 0)))
    video_values_pad = jnp.pad(video_value, ((REACH * TV_DEV, REACH * TV_DEV), (0, 0)))

    def video_part(device):
        queries = lax.dynamic_slice_in_dim(video_queries, device * TV_DEV, TV_DEV, 0)
        key_rows = lax.dynamic_slice_in_dim(audio_keys_pad, device * TA_DEV, window * TA_DEV, 0)
        values = lax.dynamic_slice_in_dim(audio_values_pad, device * TA_DEV, window * TA_DEV, 0)
        allowed = lax.dynamic_slice(row_padded, (device * audio_span, device * video_span), (window * audio_span, video_span)).T
        return attend(queries, key_rows, values, allowed)

    def audio_part(device):
        queries = lax.dynamic_slice_in_dim(audio_queries, device * TA_DEV, TA_DEV, 0)
        key_rows = lax.dynamic_slice_in_dim(video_keys_pad, device * TV_DEV, window * TV_DEV, 0)
        values = lax.dynamic_slice_in_dim(video_values_pad, device * TV_DEV, window * TV_DEV, 0)
        allowed = lax.dynamic_slice(col_padded, (device * audio_span, device * video_span), (audio_span, window * video_span))
        return attend(queries, key_rows, values, allowed)
    shards = jnp.arange(N_VIDEO, dtype=jnp.int32)
    video_mixed = lax.map(video_part, shards).reshape(NV, H * E)
    audio_mixed = lax.map(audio_part, shards).reshape(NA, H * E)
    return (video_mixed, audio_mixed)
```

```python
import math

import jax
import jax.numpy as jnp
from jax import lax
from jax.experimental import pallas as pl
from jax.experimental.pallas import tpu as pltpu
from jax.sharding import PartitionSpec as P

MESH = pl.DeviceIdType.MESH
F32 = jnp.float32
BF16 = jnp.bfloat16
E = 128
BLOCK = 128
REACH = 2
EPS = 1e-06
MASKED = -1e30
WINDOW = 2 * REACH + 1
OFFSETS = (-1, 1, -2, 2)
SCORE_SCALE = math.log2(math.e) / math.sqrt(E)
VMEM_LIMIT = 60 * 1024 * 1024


def contract_last(left, right):
    return lax.dot_general(left, right, (((1,), (1,)), ((), ())), preferred_element_type=F32)


def head(ref, h):
    return ref[:, h * E : (h + 1) * E]


def kernel(
    n_video, n_audio,
    vq_hbm, vk_hbm, vv_hbm, aq_hbm, ak_hbm, av_hbm, vqg_hbm, vkg_hbm, aqg_hbm, akg_hbm, pairs_hbm,
    vout_hbm, aout_hbm,
    vq, vk, vv, aq_raw, ak_raw, aq, ak, av, vout, aout, mask,
    sums_a, sums_a_in, sums_v, sums_v_in,
    part_o, part_s, back_o, back_s, mine_o, mine_s,
    vqg, vkg, aqg, akg, pairs,
    load_sem, out_sem, sa_send, sa_recv, sv_send, sv_recv,
    av_send, av_recv, aq_send, aq_recv, ak_send, ak_recv,
    po_send, po_recv, ps_send, ps_recv,
):
    me = lax.axis_index("video")
    mine_z = lax.axis_index("audio")
    width = vq.shape[1] * n_audio
    heads = vq.shape[1] // E
    v_blocks = vq.shape[0] // BLOCK

    def near(offset):
        return (lax.rem(me + offset + n_video, n_video), mine_z)

    def peer(step):
        return (me, lax.rem(mine_z + step, n_audio))

    loads = [
        pltpu.make_async_copy(source, target, load_sem.at[i])
        for i, (source, target) in enumerate(
            (
                (aq_hbm, aq_raw), (ak_hbm, ak_raw), (vk_hbm, vk), (vq_hbm, vq), (pairs_hbm, pairs), (aqg_hbm, aqg),
                (akg_hbm, akg), (vqg_hbm, vqg), (vkg_hbm, vkg), (vv_hbm, vv), (av_hbm, av.at[REACH]),
            )
        )
    ]
    for load in loads:
        load.start()

    barrier = pltpu.get_barrier_semaphore()
    for offset in OFFSETS:
        pl.semaphore_signal(barrier, inc=1, device_id=near(offset), device_id_type=MESH)
    for step in range(1, n_audio):
        pl.semaphore_signal(barrier, inc=1, device_id=peer(step), device_id_type=MESH)

    lane = lax.broadcasted_iota(jnp.int32, (BLOCK, 128), 1)

    def row_sums(ref, block):
        wide = ref[block * BLOCK : (block + 1) * BLOCK, :].astype(F32)
        return jnp.sum(wide * wide, axis=1, keepdims=True)

    loads[0].wait()
    loads[1].wait()
    table = jnp.where(lane == 0, row_sums(aq_raw, 0), 0.0)
    table = jnp.where(lane == 1, row_sums(ak_raw, 0), table)
    sums_a[...] = table.T[:8]

    pl.semaphore_wait(barrier, len(OFFSETS) + n_audio - 1)

    def exchange(source, into, send, recv):
        return [
            pltpu.make_async_remote_copy(
                src_ref=source, dst_ref=into.at[step - 1], send_sem=send.at[step - 1], recv_sem=recv.at[step - 1],
                device_id=peer(step), device_id_type=MESH,
            )
            for step in range(1, n_audio)
        ]

    def spread(source, into, send, recv):
        return [
            pltpu.make_async_remote_copy(
                src_ref=source, dst_ref=into.at[REACH - offset], send_sem=send.at[i], recv_sem=recv.at[REACH - offset],
                device_id=near(offset), device_id_type=MESH,
            )
            for i, offset in enumerate(OFFSETS)
        ]

    def arrived(ref, recv, slot):
        pltpu.make_async_remote_copy(
            src_ref=ref.at[slot], dst_ref=ref.at[slot], send_sem=recv.at[slot], recv_sem=recv.at[slot],
            device_id=near(1), device_id_type=MESH,
        ).wait_recv()

    sa_copies = exchange(sums_a, sums_a_in, sa_send, sa_recv)
    for copy in sa_copies:
        copy.start()
    av_copies = spread(av_hbm, av, av_send, av_recv)
    for copy in av_copies:
        copy.start()

    loads[2].wait()
    loads[3].wait()
    table = jnp.zeros((BLOCK, 128), F32)
    for block in range(v_blocks):
        table = jnp.where(lane == block, row_sums(vk, block), table)
        table = jnp.where(lane == v_blocks + block, row_sums(vq, block), table)
    sums_v[...] = table.T[: 2 * v_blocks]
    sv_copies = exchange(sums_v, sums_v_in, sv_send, sv_recv)
    for copy in sv_copies:
        copy.start()

    for load in loads[4:9]:
        load.wait()
    row_id = lax.broadcasted_iota(jnp.int32, (v_blocks, 128), 0) + me * v_blocks
    lane_id = lax.broadcasted_iota(jnp.int32, (v_blocks, 128), 1)
    low = jnp.full((v_blocks, 128), MASKED, F32)
    for slot in range(WINDOW):
        at, _ = near(slot - REACH)
        for k in range(pairs.shape[0]):
            low = jnp.where((lane_id == slot) & (row_id == pairs[k, at]), 0.0, low)
    low = jnp.where(lane_id < WINDOW, low, 0.0)
    for block in range(v_blocks):
        mask[block * BLOCK : (block + 1) * BLOCK, :] = jnp.broadcast_to(low[block : block + 1], (BLOCK, 128)).astype(BF16)

    def factors(own, arrivals, copies, rows):
        total = own[...]
        for i, copy in enumerate(copies):
            copy.wait_recv()
            total = total + arrivals[i]
        inverse = lax.rsqrt(total / width + EPS)
        return jnp.concatenate([inverse, jnp.zeros((128 - rows, 128), F32)], axis=0).T

    def normalized(block_ref, block, column, gain):
        rows = slice(block * BLOCK, (block + 1) * BLOCK)
        return (block_ref[rows, :].astype(F32) * column * gain).astype(BF16)

    gain_aq = (aqg[...] * SCORE_SCALE)[None, :]
    gain_vq = (vqg[...] * SCORE_SCALE)[None, :]
    gain_ak = akg[...][None, :]
    gain_vk = vkg[...][None, :]

    columns = factors(sums_a, sums_a_in, sa_copies, 8)
    aq[REACH] = normalized(aq_raw, 0, columns[:, 0:1], gain_aq)
    aq_copies = spread(aq.at[REACH], aq, aq_send, aq_recv)
    for copy in aq_copies:
        copy.start()
    ak[REACH] = normalized(ak_raw, 0, columns[:, 1:2], gain_ak)
    ak_copies = spread(ak.at[REACH], ak, ak_send, ak_recv)
    for copy in ak_copies:
        copy.start()

    columns = factors(sums_v, sums_v_in, sv_copies, 2 * v_blocks)
    for block in range(v_blocks):
        rows = slice(block * BLOCK, (block + 1) * BLOCK)
        vk[rows, :] = normalized(vk, block, columns[:, block : block + 1], gain_vk)
    for block in range(v_blocks):
        rows = slice(block * BLOCK, (block + 1) * BLOCK)
        at = v_blocks + block
        vq[rows, :] = normalized(vq, block, columns[:, at : at + 1], gain_vq)

    loads[9].wait()
    loads[10].wait()

    def chosen(slot):
        return jnp.where(lane == slot, 1.0, 0.0).astype(BF16)

    def blend(queries, keys, values):
        scores = contract_last(queries, keys)
        top = jnp.max(scores, axis=1, keepdims=True)
        weights = jnp.exp2(scores - top).astype(BF16)
        ones = jnp.ones(values.shape, BF16)
        mixed = jnp.dot(weights, jnp.concatenate([values, ones], axis=1), preferred_element_type=F32)
        return top, mixed[:, :E], mixed[:, E:]

    def audio_part(slot, into_o, into_s):
        logs = jnp.zeros((BLOCK, 128), F32)
        for h in range(heads):
            queries = jnp.concatenate([head(aq.at[slot], h), chosen(slot)], axis=1)
            keys = jnp.concatenate([head(vk, h), mask[...]], axis=1)
            top, mixed, total = blend(queries, keys, head(vv, h))
            into_o[:, h * E : (h + 1) * E] = (mixed / total).astype(into_o.dtype)
            logs = jnp.where(lane == h, top + jnp.log2(total), logs)
        into_s[...] = logs.T[:8]

    audio_part(REACH, mine_o, mine_s)
    part_copies = []
    for i, offset in enumerate(OFFSETS):
        slot = REACH + offset
        arrived(aq, aq_recv, slot)
        audio_part(slot, part_o.at[i], part_s.at[i])
        for source, into, send, recv in ((part_o, back_o, po_send, po_recv), (part_s, back_s, ps_send, ps_recv)):
            copy = pltpu.make_async_remote_copy(
                src_ref=source.at[i], dst_ref=into.at[REACH - offset], send_sem=send.at[i],
                recv_sem=recv.at[REACH - offset], device_id=near(offset), device_id_type=MESH,
            )
            copy.start()
            part_copies.append(copy)

    for offset in OFFSETS:
        arrived(ak, ak_recv, REACH + offset)
        arrived(av, av_recv, REACH + offset)
    out_copies = []
    for h in range(heads):
        keys = jnp.concatenate(
            [jnp.concatenate([head(ak.at[slot], h), chosen(slot)], axis=1) for slot in range(WINDOW)], axis=0
        )
        values = jnp.concatenate([head(av.at[slot], h) for slot in range(WINDOW)], axis=0)
        queries = jnp.concatenate([head(vq, h), mask[...]], axis=1)
        _, mixed, total = blend(queries, keys, values)
        vout[:, h * E : (h + 1) * E] = mixed / total
        copy = pltpu.make_async_copy(
            vout.at[:, h * E : (h + 1) * E], vout_hbm.at[:, h * E : (h + 1) * E], out_sem.at[h]
        )
        copy.start()
        out_copies.append(copy)

    for offset in OFFSETS:
        arrived(back_o, po_recv, REACH + offset)
        arrived(back_s, ps_recv, REACH + offset)
    slots = [REACH + offset for offset in OFFSETS]
    logs = jnp.concatenate(
        [mine_s[...]] + [back_s[slot] for slot in slots] + [jnp.zeros((128 - 8 * WINDOW, 128), F32)], axis=0
    ).T
    for h in range(heads):
        cols = [logs[:, 8 * i + h : 8 * i + h + 1] for i in range(WINDOW)]
        top = cols[0]
        for col in cols[1:]:
            top = jnp.maximum(top, col)
        scales = [jnp.exp2(col - top) for col in cols]
        total = scales[0]
        for scale in scales[1:]:
            total = total + scale
        mixed = scales[0] * head(mine_o, h)
        for scale, slot in zip(scales[1:], slots):
            mixed = mixed + scale * head(back_o.at[slot], h).astype(F32)
        aout[:, h * E : (h + 1) * E] = mixed / total
    copy = pltpu.make_async_copy(aout, aout_hbm, out_sem.at[heads])
    copy.start()
    out_copies.append(copy)

    for copy in sa_copies + sv_copies + av_copies + aq_copies + ak_copies + part_copies:
        copy.wait_send()
    for copy in out_copies:
        copy.wait()


def solution(mesh):
    n_video, n_audio = mesh.shape["video"], mesh.shape["audio"]

    def body(vq, vk, vv, aq, ak, av, vqg, vkg, aqg, akg, pairs):
        rows_v, wide = vq.shape
        rows_a = aq.shape[0]
        heads = wide // E
        blocks = rows_v // BLOCK
        anywhere = pl.BlockSpec(memory_space=pl.ANY)
        in_hbm = pl.BlockSpec(memory_space=pltpu.HBM)
        dma = pltpu.SemaphoreType.DMA
        near = len(OFFSETS)
        return pl.pallas_call(
            lambda *refs: kernel(n_video, n_audio, *refs),
            out_shape=(
                jax.ShapeDtypeStruct((rows_v, wide), F32),
                jax.ShapeDtypeStruct((rows_a, wide), F32),
            ),
            in_specs=[in_hbm] * 11,
            out_specs=(anywhere, anywhere),
            scratch_shapes=[
                pltpu.VMEM((rows_v, wide), BF16),
                pltpu.VMEM((rows_v, wide), BF16),
                pltpu.VMEM((rows_v, wide), BF16),
                pltpu.VMEM((rows_a, wide), BF16),
                pltpu.VMEM((rows_a, wide), BF16),
                pltpu.VMEM((WINDOW, rows_a, wide), BF16),
                pltpu.VMEM((WINDOW, rows_a, wide), BF16),
                pltpu.VMEM((WINDOW, rows_a, wide), BF16),
                pltpu.VMEM((rows_v, wide), F32),
                pltpu.VMEM((rows_a, wide), F32),
                pltpu.VMEM((rows_v, 128), BF16),
                pltpu.VMEM((8, 128), F32),
                pltpu.VMEM((n_audio - 1, 8, 128), F32),
                pltpu.VMEM((2 * blocks, 128), F32),
                pltpu.VMEM((n_audio - 1, 2 * blocks, 128), F32),
                pltpu.VMEM((near, rows_a, wide), BF16),
                pltpu.VMEM((near, 8, 128), F32),
                pltpu.VMEM((WINDOW, rows_a, wide), BF16),
                pltpu.VMEM((WINDOW, 8, 128), F32),
                pltpu.VMEM((rows_a, wide), F32),
                pltpu.VMEM((8, 128), F32),
                pltpu.VMEM((wide,), F32),
                pltpu.VMEM((wide,), F32),
                pltpu.VMEM((wide,), F32),
                pltpu.VMEM((wide,), F32),
                pltpu.SMEM(pairs.shape[::-1], jnp.int32),
                dma((11,)),
                dma((heads + 1,)),
                dma((n_audio - 1,)),
                dma((n_audio - 1,)),
                dma((n_audio - 1,)),
                dma((n_audio - 1,)),
                dma((near,)),
                dma((WINDOW,)),
                dma((near,)),
                dma((WINDOW,)),
                dma((near,)),
                dma((WINDOW,)),
                dma((near,)),
                dma((WINDOW,)),
                dma((near,)),
                dma((WINDOW,)),
            ],
            compiler_params=pltpu.CompilerParams(
                collective_id=0, has_side_effects=True, vmem_limit_bytes=VMEM_LIMIT
            ),
            name="paired_attention",
        )(vq, vk, vv, aq, ak, av, vqg, vkg, aqg, akg, pairs.T)

    both = P("video", "audio")
    return jax.shard_map(
        body,
        mesh=mesh,
        in_specs=(both,) * 6 + (P("audio"),) * 4 + (P(),),
        out_specs=(both, both),
        check_vma=False,
    )
```

```python
import math

import jax
import jax.numpy as jnp
from jax import lax
from jax.experimental import pallas as pl
from jax.experimental.pallas import tpu as pltpu
from jax.sharding import PartitionSpec as P

MESH = pl.DeviceIdType.MESH
F32 = jnp.float32
BF16 = jnp.bfloat16
E = 128
BLOCK = 128
EPS = 1e-06
MASKED = -1e30
SCORE_SCALE = math.log2(math.e) / math.sqrt(E)
VMEM_LIMIT = 60 * 1024 * 1024

PLACES = (0, -1, 1, 2, -2)
WINDOW = len(PLACES)
MIRROR = (0, 1, 2, 4, 3)
OTHER, BESIDE, AHEAD, BEHIND = range(1, WINDOW)
STEPS = (1, 2, -1, -2)


def contract_last(left, right):
    return lax.dot_general(left, right, (((1,), (1,)), ((), ())), preferred_element_type=F32)


def head(ref, h):
    return ref[:, h * E : (h + 1) * E]


def kernel(
    n_video, n_audio,
    vq_hbm, vk_hbm, vv_hbm, aq_hbm, ak_hbm, av_hbm, vqg_hbm, vkg_hbm, aqg_hbm, akg_hbm, pairs_hbm,
    vout, aout,
    vq, vk, vv, aq, ak, av, mask, scores_a, scores_v,
    sums_a, sums_a_in, sums_a_on, sums_a_far, sums_v, sums_v_in, sums_v_on, sums_v_far, factors_a,
    part_o, part_s, back_o, back_s, mine_o, mine_s,
    vqg, vkg, aqg, akg, pairs,
    load_sem, sa_send, sa_recv, sa_far_send, sa_far_recv, sv_send, sv_recv, sv_far_send, sv_far_recv, fa_send, fa_recv,
    aq_send, aq_recv, ak_send, ak_recv, av_send, av_recv,
    po_send, po_recv, ps_send, ps_recv,
):
    me = lax.axis_index("video")
    mine_z = lax.axis_index("audio")
    side = 2 * lax.rem(me, 2) - 1
    width = vq.shape[1] * n_audio
    heads = vq.shape[1] // E
    v_blocks = vq.shape[0] // BLOCK

    def at(place):
        return lax.rem(me + PLACES[place] * side + n_video, n_video)

    def near(place):
        return (at(place), mine_z)

    def peer(step):
        return (me, lax.rem(mine_z + step + n_audio, n_audio))

    loads = [
        pltpu.make_async_copy(source, target, load_sem.at[i])
        for i, (source, target) in enumerate(
            (
                (aq_hbm, aq.at[0]), (ak_hbm, ak.at[0]), (vk_hbm, vk), (vq_hbm, vq), (pairs_hbm, pairs), (aqg_hbm, aqg),
                (akg_hbm, akg), (vqg_hbm, vqg), (vkg_hbm, vkg), (vv_hbm, vv), (av_hbm, av.at[0]),
            )
        )
    ]
    loads[0].start()
    loads[1].start()
    barrier = pltpu.get_barrier_semaphore()
    for place in range(1, WINDOW):
        pl.semaphore_signal(barrier, inc=1, device_id=near(place), device_id_type=MESH)
    for step in STEPS:
        pl.semaphore_signal(barrier, inc=1, device_id=peer(step), device_id_type=MESH)
    for load in loads[2:]:
        load.start()

    lane = lax.broadcasted_iota(jnp.int32, (BLOCK, 128), 1)

    def row_sums(rows):
        wide = rows.astype(F32)
        return jnp.sum(wide * wide, axis=1, keepdims=True)

    loads[0].wait()
    loads[1].wait()
    table = jnp.where(lane == 0, row_sums(aq[0]), 0.0)
    table = jnp.where(lane == 1, row_sums(ak[0]), table)
    sums_a[...] = table.T[:2]

    pl.semaphore_wait(barrier, WINDOW - 1 + len(STEPS))

    sent = []

    def push(source, into, slot, send, recv, place):
        copy = pltpu.make_async_remote_copy(
            src_ref=source, dst_ref=into.at[slot], send_sem=send, recv_sem=recv.at[slot],
            device_id=near(place), device_id_type=MESH,
        )
        copy.start()
        sent.append(copy)

    def exchange(source, into, send, recv):
        copies = [
            pltpu.make_async_remote_copy(
                src_ref=source, dst_ref=into.at[STEPS.index(-step)], send_sem=send.at[i], recv_sem=recv.at[STEPS.index(-step)],
                device_id=peer(step), device_id_type=MESH,
            )
            for i, step in enumerate(STEPS)
        ]
        for copy in copies:
            copy.start()
        sent.extend(copies)
        return copies

    def pass_on(arrivals, copies, on, far, send, recv):
        for copy in copies:
            copy.wait_recv()
        on[...] = arrivals[STEPS.index(1)] + arrivals[STEPS.index(2)]
        copies = [
            pltpu.make_async_remote_copy(
                src_ref=source, dst_ref=far.at[i], send_sem=send.at[i], recv_sem=recv.at[i],
                device_id=peer(step), device_id_type=MESH,
            )
            for i, (source, step) in enumerate(((on, -2), (arrivals.at[STEPS.index(-1)], 2)))
        ]
        for copy in copies:
            copy.start()
        sent.extend(copies)
        return copies

    def factors(own, arrivals, far, copies):
        total = own[...]
        for i in range(len(STEPS)):
            total = total + arrivals[i]
        for i, copy in enumerate(copies):
            copy.wait_recv()
            total = total + far[i]
        return lax.rsqrt(total / width + EPS)

    def spread(source, into, send, recv):
        for i, place in enumerate((AHEAD, BEHIND, OTHER)):
            push(source, into, MIRROR[place], send.at[i], recv, place)

    def arrived(ref, recv, slot):
        pltpu.make_async_remote_copy(
            src_ref=ref.at[slot], dst_ref=ref.at[slot], send_sem=recv.at[slot], recv_sem=recv.at[slot],
            device_id=near(OTHER), device_id_type=MESH,
        ).wait_recv()

    def relay(ref, send, recv):
        arrived(ref, recv, BEHIND)
        push(ref.at[BEHIND], ref, BESIDE, send.at[3], recv, OTHER)

    sa_copies = exchange(sums_a, sums_a_in, sa_send, sa_recv)
    spread(aq_hbm, aq, aq_send, aq_recv)
    spread(ak_hbm, ak, ak_send, ak_recv)
    spread(av_hbm, av, av_send, av_recv)

    loads[2].wait()
    loads[3].wait()
    table = jnp.zeros((BLOCK, 128), F32)
    for block in range(v_blocks):
        rows = slice(block * BLOCK, (block + 1) * BLOCK)
        table = jnp.where(lane == block, row_sums(vk[rows, :]), table)
        table = jnp.where(lane == v_blocks + block, row_sums(vq[rows, :]), table)
    sums_v[...] = table.T[: 2 * v_blocks]
    sv_copies = exchange(sums_v, sums_v_in, sv_send, sv_recv)

    for load in loads[4:]:
        load.wait()
    row_id = lax.broadcasted_iota(jnp.int32, (v_blocks, 128), 0) + me * v_blocks
    lane_id = lax.broadcasted_iota(jnp.int32, (v_blocks, 128), 1)
    low = jnp.full((v_blocks, 128), MASKED, F32)
    for place in range(WINDOW):
        where = at(place)
        for k in range(pairs.shape[0]):
            low = jnp.where((lane_id == place) & (row_id == pairs[k, where]), 0.0, low)
    low = jnp.where(lane_id < WINDOW, low, 0.0)
    for block in range(v_blocks):
        mask[block * BLOCK : (block + 1) * BLOCK, :] = jnp.broadcast_to(low[block : block + 1], (BLOCK, 128)).astype(BF16)

    gain_a = (aqg[...] * vkg[...] * SCORE_SCALE)[None, :]
    gain_v = (vqg[...] * akg[...] * SCORE_SCALE)[None, :]
    vq[...] = (vq[...].astype(F32) * gain_v).astype(BF16)

    def chosen(place):
        return jnp.where(lane == place, 1.0, 0.0).astype(BF16)

    def marked(rows, place):
        return jnp.concatenate([rows, chosen(place)], axis=1)

    def span(places):
        return slice(places[0] * BLOCK, (places[-1] + 1) * BLOCK)

    def audio_scores(places):
        for h in range(heads):
            queries = jnp.concatenate(
                [marked((head(aq.at[place], h).astype(F32) * head(gain_a, h)).astype(BF16), place) for place in places], axis=0
            )
            keys = jnp.concatenate([head(vk, h), mask[...]], axis=1)
            scores_a[h, span(places), :] = contract_last(queries, keys)

    def video_scores(places):
        for h in range(heads):
            keys = jnp.concatenate([marked(head(ak.at[place], h), place) for place in places], axis=0)
            queries = jnp.concatenate([head(vq, h), mask[...]], axis=1)
            scores_v[h, :, span(places)] = contract_last(queries, keys)

    def blend(scores, key_scale, query_scale, values):
        scores = scores * key_scale
        top = jnp.max(scores, axis=1, keepdims=True)
        weights = jnp.exp2((scores - top) * query_scale).astype(BF16)
        ones = jnp.ones(values.shape, BF16)
        mixed = jnp.dot(weights, jnp.concatenate([values, ones], axis=1), preferred_element_type=F32)
        return top * query_scale, mixed[:, :E], mixed[:, E:]

    def as_columns(pieces):
        rows = sum(piece.shape[0] for piece in pieces)
        return jnp.concatenate(list(pieces) + [jnp.zeros((128 - rows, 128), F32)], axis=0).T

    sa_copies = pass_on(sums_a_in, sa_copies, sums_a_on, sums_a_far, sa_far_send, sa_far_recv)
    audio_scores((0,))
    video_scores((0,))
    relay(aq, aq_send, aq_recv)
    sv_copies = pass_on(sums_v_in, sv_copies, sums_v_on, sums_v_far, sv_far_send, sv_far_recv)
    factors_a[0] = factors(sums_a, sums_a_in, sums_a_far, sa_copies)
    for place in (AHEAD, BEHIND, BESIDE, OTHER):
        push(factors_a.at[0], factors_a, MIRROR[place], fa_send.at[place - 1], fa_recv, place)

    arrived(aq, aq_recv, AHEAD)
    audio_scores((AHEAD, BEHIND))
    arrived(ak, ak_recv, AHEAD)
    relay(ak, ak_send, ak_recv)
    for place in (OTHER, BESIDE):
        arrived(aq, aq_recv, place)
    audio_scores((OTHER, BESIDE))
    video_scores((AHEAD, BEHIND))
    relay(av, av_send, av_recv)

    factors_v = factors(sums_v, sums_v_in, sums_v_far, sv_copies)
    scale_k = jnp.concatenate([factors_v[block : block + 1] for block in range(v_blocks)], axis=1)

    def audio_part(places):
        columns = as_columns([factors_a[place] for place in places])
        query_scale = jnp.concatenate([columns[:, 2 * i : 2 * i + 1] for i in range(len(places))], axis=0)
        logs = [jnp.zeros((BLOCK, 128), F32) for _ in places]
        for h in range(heads):
            top, mixed, total = blend(scores_a[h, span(places), :], scale_k, query_scale, head(vv, h))
            result = mixed / total
            log = top + jnp.log2(total)
            for i, place in enumerate(places):
                rows = slice(i * BLOCK, (i + 1) * BLOCK)
                logs[i] = jnp.where(lane == h, log[rows], logs[i])
                if place == 0:
                    mine_o[h] = result[rows]
                else:
                    part_o[place - 1, h] = result[rows].astype(BF16)
        for i, place in enumerate(places):
            if place == 0:
                mine_s[...] = logs[i].T[:8]
            else:
                part_s[place - 1] = logs[i].T[:8]
                push(part_o.at[place - 1], back_o, MIRROR[place], po_send.at[place - 1], po_recv, place)
                push(part_s.at[place - 1], back_s, MIRROR[place], ps_send.at[place - 1], ps_recv, place)

    audio_part((0,))
    arrived(factors_a, fa_recv, AHEAD)
    arrived(factors_a, fa_recv, BEHIND)
    audio_part((AHEAD, BEHIND))
    arrived(factors_a, fa_recv, OTHER)
    arrived(factors_a, fa_recv, BESIDE)
    audio_part((OTHER, BESIDE))

    for place in (OTHER, BESIDE):
        arrived(ak, ak_recv, place)
    video_scores((OTHER, BESIDE))
    for place in (OTHER, AHEAD, BESIDE):
        arrived(av, av_recv, place)
    scale_a = jnp.concatenate([factors_a[place, 1:2] for place in range(WINDOW)], axis=1)
    columns_v = as_columns([factors_v[v_blocks:]])
    query_scale = jnp.concatenate([columns_v[:, block : block + 1] for block in range(v_blocks)], axis=0)
    for h in range(heads):
        values = jnp.concatenate([head(av.at[place], h) for place in range(WINDOW)], axis=0)
        _, mixed, total = blend(scores_v[h], scale_a, query_scale, values)
        vout[:, h * E : (h + 1) * E] = mixed / total

    for place in range(1, WINDOW):
        arrived(back_s, ps_recv, place)
        arrived(back_o, po_recv, place)
    logs = as_columns([mine_s[...]] + [back_s[place] for place in range(1, WINDOW)])
    for h in range(heads):
        cols = [logs[:, 8 * i + h : 8 * i + h + 1] for i in range(WINDOW)]
        top = cols[0]
        for col in cols[1:]:
            top = jnp.maximum(top, col)
        scales = [jnp.exp2(col - top) for col in cols]
        total = scales[0]
        for scale in scales[1:]:
            total = total + scale
        mixed = scales[0] * mine_o[h]
        for place in range(1, WINDOW):
            mixed = mixed + scales[place] * back_o[place, h].astype(F32)
        aout[:, h * E : (h + 1) * E] = mixed / total

    for copy in sent:
        copy.wait_send()


def solution(mesh):
    n_video, n_audio = mesh.shape["video"], mesh.shape["audio"]

    def body(vq, vk, vv, aq, ak, av, vqg, vkg, aqg, akg, pairs):
        rows_v, wide = vq.shape
        rows_a = aq.shape[0]
        blocks = rows_v // BLOCK
        heads = wide // E
        in_hbm = pl.BlockSpec(memory_space=pltpu.HBM)
        in_vmem = pl.BlockSpec(memory_space=pltpu.VMEM)
        dma = pltpu.SemaphoreType.DMA
        near = WINDOW - 1
        return pl.pallas_call(
            lambda *refs: kernel(n_video, n_audio, *refs),
            out_shape=(pltpu.VMEM((rows_v, wide), F32), pltpu.VMEM((rows_a, wide), F32)),
            in_specs=[in_hbm] * 11,
            out_specs=(in_vmem, in_vmem),
            scratch_shapes=[
                pltpu.VMEM((rows_v, wide), BF16),
                pltpu.VMEM((rows_v, wide), BF16),
                pltpu.VMEM((rows_v, wide), BF16),
                pltpu.VMEM((WINDOW, rows_a, wide), BF16),
                pltpu.VMEM((WINDOW, rows_a, wide), BF16),
                pltpu.VMEM((WINDOW, rows_a, wide), BF16),
                pltpu.VMEM((rows_v, 128), BF16),
                pltpu.VMEM((heads, WINDOW * rows_a, rows_v), F32),
                pltpu.VMEM((heads, rows_v, WINDOW * rows_a), F32),
                pltpu.VMEM((2, 128), F32),
                pltpu.VMEM((len(STEPS), 2, 128), F32),
                pltpu.VMEM((2, 128), F32),
                pltpu.VMEM((2, 2, 128), F32),
                pltpu.VMEM((2 * blocks, 128), F32),
                pltpu.VMEM((len(STEPS), 2 * blocks, 128), F32),
                pltpu.VMEM((2 * blocks, 128), F32),
                pltpu.VMEM((2, 2 * blocks, 128), F32),
                pltpu.VMEM((WINDOW, 2, 128), F32),
                pltpu.VMEM((near, heads, rows_a, E), BF16),
                pltpu.VMEM((near, 8, 128), F32),
                pltpu.VMEM((WINDOW, heads, rows_a, E), BF16),
                pltpu.VMEM((WINDOW, 8, 128), F32),
                pltpu.VMEM((heads, rows_a, E), F32),
                pltpu.VMEM((8, 128), F32),
                pltpu.VMEM((wide,), F32),
                pltpu.VMEM((wide,), F32),
                pltpu.VMEM((wide,), F32),
                pltpu.VMEM((wide,), F32),
                pltpu.SMEM(pairs.shape[::-1], jnp.int32),
                dma((11,)),
                dma((len(STEPS),)),
                dma((len(STEPS),)),
                dma((2,)),
                dma((2,)),
                dma((len(STEPS),)),
                dma((len(STEPS),)),
                dma((2,)),
                dma((2,)),
                dma((near,)),
                dma((WINDOW,)),
                dma((near,)),
                dma((WINDOW,)),
                dma((near,)),
                dma((WINDOW,)),
                dma((near,)),
                dma((WINDOW,)),
                dma((near,)),
                dma((WINDOW,)),
                dma((near,)),
                dma((WINDOW,)),
            ],
            compiler_params=pltpu.CompilerParams(
                collective_id=0, has_side_effects=True, vmem_limit_bytes=VMEM_LIMIT
            ),
            name="paired_attention",
        )(vq, vk, vv, aq, ak, av, vqg, vkg, aqg, akg, pairs.T)

    both = P("video", "audio")
    return jax.shard_map(
        body,
        mesh=mesh,
        in_specs=(both,) * 6 + (P("audio"),) * 4 + (P(),),
        out_specs=(both, both),
        check_vma=False,
    )
```

```python
import math

import jax
import jax.numpy as jnp
from jax import lax
from jax.experimental import pallas as pl
from jax.experimental.pallas import tpu as pltpu
from jax.sharding import PartitionSpec as P

MESH = pl.DeviceIdType.MESH
F32 = jnp.float32
BF16 = jnp.bfloat16
E = 128
BLOCK = 128
EPS = 1e-06
MASKED = -1e30
SCORE_SCALE = math.log2(math.e) / math.sqrt(E)
VMEM_LIMIT = 60 * 1024 * 1024

PLACES = (0, -1, 1, 2, -2)
WINDOW = len(PLACES)
MIRROR = (0, 1, 2, 4, 3)
OTHER, BESIDE, AHEAD, BEHIND = range(1, WINDOW)
STEPS = (1, 2, -1, -2)


def contract_last(left, right):
    return lax.dot_general(left, right, (((1,), (1,)), ((), ())), preferred_element_type=F32)


def head(ref, h):
    return ref[:, h * E : (h + 1) * E]


def kernel(
    n_video, n_audio,
    vq_hbm, vk_hbm, vv_hbm, aq_hbm, ak_hbm, av_hbm, vqg_hbm, vkg_hbm, aqg_hbm, akg_hbm, pairs_hbm,
    vout, aout,
    vq, vk, vv, aq, ak, av, mask, scores_a, scores_v,
    sums_a, sums_a_in, sums_a_on, sums_a_far, sums_v, sums_v_in, sums_v_on, sums_v_far, factors_a,
    part_o, part_s, back_o, back_s, mine_o, mine_s,
    vqg, vkg, aqg, akg, pairs,
    load_sem, sa_send, sa_recv, sa_far_send, sa_far_recv, sv_send, sv_recv, sv_far_send, sv_far_recv, fa_send, fa_recv,
    aq_send, aq_recv, ak_send, ak_recv, av_send, av_recv,
    po_send, po_recv, ps_send, ps_recv,
):
    me = lax.axis_index("video")
    mine_z = lax.axis_index("audio")
    side = 2 * lax.rem(me, 2) - 1
    width = vq.shape[1] * n_audio
    heads = vq.shape[1] // E
    v_blocks = vq.shape[0] // BLOCK

    def at(place):
        return lax.rem(me + PLACES[place] * side + n_video, n_video)

    def near(place):
        return (at(place), mine_z)

    def peer(step):
        return (me, lax.rem(mine_z + step + n_audio, n_audio))

    loads = [
        pltpu.make_async_copy(source, target, load_sem.at[i])
        for i, (source, target) in enumerate(
            (
                (aq_hbm, aq.at[0]), (ak_hbm, ak.at[0]), (vk_hbm, vk), (vq_hbm, vq), (pairs_hbm, pairs), (aqg_hbm, aqg),
                (akg_hbm, akg), (vqg_hbm, vqg), (vkg_hbm, vkg), (vv_hbm, vv), (av_hbm, av.at[0]),
            )
        )
    ]
    loads[0].start()
    loads[1].start()
    barrier = pltpu.get_barrier_semaphore()
    for place in range(1, WINDOW):
        pl.semaphore_signal(barrier, inc=1, device_id=near(place), device_id_type=MESH)
    for step in STEPS:
        pl.semaphore_signal(barrier, inc=1, device_id=peer(step), device_id_type=MESH)
    for load in loads[2:]:
        load.start()

    lane = lax.broadcasted_iota(jnp.int32, (BLOCK, 128), 1)

    def row_sums(rows):
        wide = rows.astype(F32)
        return jnp.sum(wide * wide, axis=1, keepdims=True)

    loads[0].wait()
    loads[1].wait()
    table = jnp.where(lane == 0, row_sums(aq[0]), 0.0)
    table = jnp.where(lane == 1, row_sums(ak[0]), table)
    sums_a[...] = table.T[:2]

    pl.semaphore_wait(barrier, WINDOW - 1 + len(STEPS))

    sent = []

    def push(source, into, slot, send, recv, place):
        copy = pltpu.make_async_remote_copy(
            src_ref=source, dst_ref=into.at[slot], send_sem=send, recv_sem=recv.at[slot],
            device_id=near(place), device_id_type=MESH,
        )
        copy.start()
        sent.append(copy)

    def exchange(source, into, send, recv):
        copies = [
            pltpu.make_async_remote_copy(
                src_ref=source, dst_ref=into.at[STEPS.index(-step)], send_sem=send.at[i], recv_sem=recv.at[STEPS.index(-step)],
                device_id=peer(step), device_id_type=MESH,
            )
            for i, step in enumerate(STEPS)
        ]
        for copy in copies:
            copy.start()
        sent.extend(copies)
        return copies

    def pass_on(arrivals, copies, on, far, send, recv):
        for copy in copies:
            copy.wait_recv()
        on[...] = arrivals[STEPS.index(1)] + arrivals[STEPS.index(2)]
        copies = [
            pltpu.make_async_remote_copy(
                src_ref=source, dst_ref=far.at[i], send_sem=send.at[i], recv_sem=recv.at[i],
                device_id=peer(step), device_id_type=MESH,
            )
            for i, (source, step) in enumerate(((on, -2), (arrivals.at[STEPS.index(-1)], 2)))
        ]
        for copy in copies:
            copy.start()
        sent.extend(copies)
        return copies

    def factors(own, arrivals, far, copies):
        total = own[...]
        for i in range(len(STEPS)):
            total = total + arrivals[i]
        for i, copy in enumerate(copies):
            copy.wait_recv()
            total = total + far[i]
        return lax.rsqrt(total / width + EPS)

    def spread(source, into, send, recv):
        for i, place in enumerate((AHEAD, BEHIND, OTHER)):
            push(source, into, MIRROR[place], send.at[i], recv, place)

    def arrived(ref, recv, slot):
        pltpu.make_async_remote_copy(
            src_ref=ref.at[slot], dst_ref=ref.at[slot], send_sem=recv.at[slot], recv_sem=recv.at[slot],
            device_id=near(OTHER), device_id_type=MESH,
        ).wait_recv()

    def relay(ref, send, recv):
        arrived(ref, recv, BEHIND)
        push(ref.at[BEHIND], ref, BESIDE, send.at[3], recv, OTHER)

    sa_copies = exchange(sums_a, sums_a_in, sa_send, sa_recv)
    spread(aq_hbm, aq, aq_send, aq_recv)
    spread(ak_hbm, ak, ak_send, ak_recv)
    spread(av_hbm, av, av_send, av_recv)

    loads[2].wait()
    loads[3].wait()
    table = jnp.zeros((BLOCK, 128), F32)
    for block in range(v_blocks):
        rows = slice(block * BLOCK, (block + 1) * BLOCK)
        table = jnp.where(lane == block, row_sums(vk[rows, :]), table)
        table = jnp.where(lane == v_blocks + block, row_sums(vq[rows, :]), table)
    sums_v[...] = table.T[: 2 * v_blocks]
    sv_copies = exchange(sums_v, sums_v_in, sv_send, sv_recv)

    for load in loads[4:]:
        load.wait()
    row_id = lax.broadcasted_iota(jnp.int32, (v_blocks, 128), 0) + me * v_blocks
    lane_id = lax.broadcasted_iota(jnp.int32, (v_blocks, 128), 1)
    low = jnp.full((v_blocks, 128), MASKED, F32)
    for place in range(WINDOW):
        where = at(place)
        for k in range(pairs.shape[0]):
            low = jnp.where((lane_id == place) & (row_id == pairs[k, where]), 0.0, low)
    low = jnp.where(lane_id < WINDOW, low, 0.0)
    for block in range(v_blocks):
        mask[block * BLOCK : (block + 1) * BLOCK, :] = jnp.broadcast_to(low[block : block + 1], (BLOCK, 128)).astype(BF16)

    gain_a = (aqg[...] * vkg[...] * SCORE_SCALE)[None, :]
    gain_v = (vqg[...] * akg[...] * SCORE_SCALE)[None, :]
    vq[...] = (vq[...].astype(F32) * gain_v).astype(BF16)

    def chosen(place):
        return jnp.where(lane == place, 1.0, 0.0).astype(BF16)

    def marked(rows, place):
        return jnp.concatenate([rows, chosen(place)], axis=1)

    def span(places):
        return slice(places[0] * BLOCK, (places[-1] + 1) * BLOCK)

    def audio_scores(places):
        for h in range(heads):
            queries = jnp.concatenate(
                [marked((head(aq.at[place], h).astype(F32) * head(gain_a, h)).astype(BF16), place) for place in places], axis=0
            )
            keys = jnp.concatenate([head(vk, h), mask[...]], axis=1)
            scores_a[h, span(places), :] = contract_last(queries, keys)

    def video_scores(places):
        for h in range(heads):
            keys = jnp.concatenate([marked(head(ak.at[place], h), place) for place in places], axis=0)
            queries = jnp.concatenate([head(vq, h), mask[...]], axis=1)
            scores_v[h, :, span(places)] = contract_last(queries, keys)

    def blend(scores, top, query_scale, values):
        weights = jnp.exp2((scores - top) * query_scale).astype(BF16)
        ones = jnp.ones(values.shape, BF16)
        mixed = jnp.dot(weights, jnp.concatenate([values, ones], axis=1), preferred_element_type=F32)
        return top * query_scale, mixed[:, :E], mixed[:, E:]

    def as_columns(pieces):
        rows = sum(piece.shape[0] for piece in pieces)
        return jnp.concatenate(list(pieces) + [jnp.zeros((128 - rows, 128), F32)], axis=0).T

    sa_copies = pass_on(sums_a_in, sa_copies, sums_a_on, sums_a_far, sa_far_send, sa_far_recv)
    audio_scores((0,))
    video_scores((0,))
    relay(aq, aq_send, aq_recv)
    sv_copies = pass_on(sums_v_in, sv_copies, sums_v_on, sums_v_far, sv_far_send, sv_far_recv)
    factors_a[0] = factors(sums_a, sums_a_in, sums_a_far, sa_copies)
    for place in (AHEAD, BEHIND, BESIDE, OTHER):
        push(factors_a.at[0], factors_a, MIRROR[place], fa_send.at[place - 1], fa_recv, place)

    arrived(aq, aq_recv, AHEAD)
    audio_scores((AHEAD, BEHIND))
    arrived(ak, ak_recv, AHEAD)
    relay(ak, ak_send, ak_recv)
    for place in (OTHER, BESIDE):
        arrived(aq, aq_recv, place)
    audio_scores((OTHER, BESIDE))
    video_scores((AHEAD, BEHIND))

    factors_v = factors(sums_v, sums_v_in, sums_v_far, sv_copies)
    scale_k = jnp.concatenate([factors_v[block : block + 1] for block in range(v_blocks)], axis=1)

    def audio_tops(places):
        tops = []
        for h in range(heads):
            scaled = scores_a[h, span(places), :] * scale_k
            scores_a[h, span(places), :] = scaled
            tops.append(jnp.max(scaled, axis=1, keepdims=True))
        return tops

    def audio_part(places, tops):
        columns = as_columns([factors_a[place] for place in places])
        query_scale = jnp.concatenate([columns[:, 2 * i : 2 * i + 1] for i in range(len(places))], axis=0)
        logs = [jnp.zeros((BLOCK, 128), F32) for _ in places]
        for h in range(heads):
            top, mixed, total = blend(scores_a[h, span(places), :], tops[h], query_scale, head(vv, h))
            result = mixed / total
            log = top + jnp.log2(total)
            for i, place in enumerate(places):
                rows = slice(i * BLOCK, (i + 1) * BLOCK)
                logs[i] = jnp.where(lane == h, log[rows], logs[i])
                if place == 0:
                    mine_o[h] = result[rows]
                else:
                    part_o[place - 1, h] = result[rows].astype(BF16)
        for i, place in enumerate(places):
            if place == 0:
                mine_s[...] = logs[i].T[:8]
            else:
                part_s[place - 1] = logs[i].T[:8]
                push(part_o.at[place - 1], back_o, MIRROR[place], po_send.at[place - 1], po_recv, place)
                push(part_s.at[place - 1], back_s, MIRROR[place], ps_send.at[place - 1], ps_recv, place)

    audio_part((0,), audio_tops((0,)))
    tops_far = audio_tops((AHEAD, BEHIND))
    tops_near = audio_tops((OTHER, BESIDE))
    relay(av, av_send, av_recv)
    arrived(factors_a, fa_recv, AHEAD)
    arrived(factors_a, fa_recv, BEHIND)
    audio_part((AHEAD, BEHIND), tops_far)
    arrived(factors_a, fa_recv, OTHER)
    arrived(factors_a, fa_recv, BESIDE)
    audio_part((OTHER, BESIDE), tops_near)

    for place in (OTHER, BESIDE):
        arrived(ak, ak_recv, place)
    video_scores((OTHER, BESIDE))
    for place in (OTHER, AHEAD, BESIDE):
        arrived(av, av_recv, place)
    scale_a = jnp.concatenate([factors_a[place, 1:2] for place in range(WINDOW)], axis=1)
    columns_v = as_columns([factors_v[v_blocks:]])
    query_scale = jnp.concatenate([columns_v[:, block : block + 1] for block in range(v_blocks)], axis=0)
    for h in range(heads):
        values = jnp.concatenate([head(av.at[place], h) for place in range(WINDOW)], axis=0)
        scaled = scores_v[h] * scale_a
        _, mixed, total = blend(scaled, jnp.max(scaled, axis=1, keepdims=True), query_scale, values)
        vout[:, h * E : (h + 1) * E] = mixed / total

    for place in range(1, WINDOW):
        arrived(back_s, ps_recv, place)
        arrived(back_o, po_recv, place)
    logs = as_columns([mine_s[...]] + [back_s[place] for place in range(1, WINDOW)])
    for h in range(heads):
        cols = [logs[:, 8 * i + h : 8 * i + h + 1] for i in range(WINDOW)]
        top = cols[0]
        for col in cols[1:]:
            top = jnp.maximum(top, col)
        scales = [jnp.exp2(col - top) for col in cols]
        total = scales[0]
        for scale in scales[1:]:
            total = total + scale
        mixed = scales[0] * mine_o[h]
        for place in range(1, WINDOW):
            mixed = mixed + scales[place] * back_o[place, h].astype(F32)
        aout[:, h * E : (h + 1) * E] = mixed / total

    for copy in sent:
        copy.wait_send()


def solution(mesh):
    n_video, n_audio = mesh.shape["video"], mesh.shape["audio"]

    def body(vq, vk, vv, aq, ak, av, vqg, vkg, aqg, akg, pairs):
        rows_v, wide = vq.shape
        rows_a = aq.shape[0]
        blocks = rows_v // BLOCK
        heads = wide // E
        in_hbm = pl.BlockSpec(memory_space=pltpu.HBM)
        in_vmem = pl.BlockSpec(memory_space=pltpu.VMEM)
        dma = pltpu.SemaphoreType.DMA
        near = WINDOW - 1
        return pl.pallas_call(
            lambda *refs: kernel(n_video, n_audio, *refs),
            out_shape=(pltpu.VMEM((rows_v, wide), F32), pltpu.VMEM((rows_a, wide), F32)),
            in_specs=[in_hbm] * 11,
            out_specs=(in_vmem, in_vmem),
            scratch_shapes=[
                pltpu.VMEM((rows_v, wide), BF16),
                pltpu.VMEM((rows_v, wide), BF16),
                pltpu.VMEM((rows_v, wide), BF16),
                pltpu.VMEM((WINDOW, rows_a, wide), BF16),
                pltpu.VMEM((WINDOW, rows_a, wide), BF16),
                pltpu.VMEM((WINDOW, rows_a, wide), BF16),
                pltpu.VMEM((rows_v, 128), BF16),
                pltpu.VMEM((heads, WINDOW * rows_a, rows_v), F32),
                pltpu.VMEM((heads, rows_v, WINDOW * rows_a), F32),
                pltpu.VMEM((2, 128), F32),
                pltpu.VMEM((len(STEPS), 2, 128), F32),
                pltpu.VMEM((2, 128), F32),
                pltpu.VMEM((2, 2, 128), F32),
                pltpu.VMEM((2 * blocks, 128), F32),
                pltpu.VMEM((len(STEPS), 2 * blocks, 128), F32),
                pltpu.VMEM((2 * blocks, 128), F32),
                pltpu.VMEM((2, 2 * blocks, 128), F32),
                pltpu.VMEM((WINDOW, 2, 128), F32),
                pltpu.VMEM((near, heads, rows_a, E), BF16),
                pltpu.VMEM((near, 8, 128), F32),
                pltpu.VMEM((WINDOW, heads, rows_a, E), BF16),
                pltpu.VMEM((WINDOW, 8, 128), F32),
                pltpu.VMEM((heads, rows_a, E), F32),
                pltpu.VMEM((8, 128), F32),
                pltpu.VMEM((wide,), F32),
                pltpu.VMEM((wide,), F32),
                pltpu.VMEM((wide,), F32),
                pltpu.VMEM((wide,), F32),
                pltpu.SMEM(pairs.shape[::-1], jnp.int32),
                dma((11,)),
                dma((len(STEPS),)),
                dma((len(STEPS),)),
                dma((2,)),
                dma((2,)),
                dma((len(STEPS),)),
                dma((len(STEPS),)),
                dma((2,)),
                dma((2,)),
                dma((near,)),
                dma((WINDOW,)),
                dma((near,)),
                dma((WINDOW,)),
                dma((near,)),
                dma((WINDOW,)),
                dma((near,)),
                dma((WINDOW,)),
                dma((near,)),
                dma((WINDOW,)),
                dma((near,)),
                dma((WINDOW,)),
            ],
            compiler_params=pltpu.CompilerParams(
                collective_id=0, has_side_effects=True, vmem_limit_bytes=VMEM_LIMIT
            ),
            name="paired_attention",
        )(vq, vk, vv, aq, ak, av, vqg, vkg, aqg, akg, pairs.T)

    both = P("video", "audio")
    return jax.shard_map(
        body,
        mesh=mesh,
        in_specs=(both,) * 6 + (P("audio"),) * 4 + (P(),),
        out_specs=(both, both),
        check_vma=False,
    )
```

```python
import math

import jax
import jax.numpy as jnp
from jax import lax
from jax.experimental import pallas as pl
from jax.experimental.pallas import tpu as pltpu
from jax.sharding import PartitionSpec as P

MESH = pl.DeviceIdType.MESH
F32 = jnp.float32
BF16 = jnp.bfloat16
E = 128
BLOCK = 128
EPS = 1e-06
MASKED = -1e30
SCORE_SCALE = math.log2(math.e) / math.sqrt(E)
VMEM_LIMIT = 60 * 1024 * 1024

PLACES = (0, -1, 1, 2, -2)
WINDOW = len(PLACES)
MIRROR = (0, 1, 2, 4, 3)
OTHER, BESIDE, AHEAD, BEHIND = range(1, WINDOW)
STEPS = (1, 2, -1, -2)
PARTS = 2


def contract_last(left, right):
    return lax.dot_general(left, right, (((1,), (1,)), ((), ())), preferred_element_type=F32)


def head(ref, h):
    return ref[:, h * E : (h + 1) * E]


def kernel(
    n_video, n_audio,
    vq_hbm, vk_hbm, vv_hbm, aq_hbm, ak_hbm, av_hbm, vqg_hbm, vkg_hbm, aqg_hbm, akg_hbm, pairs_hbm,
    vout, aout,
    vq, vk, vv, aq, ak, av, mask, scores_a, scores_v,
    sums_a, sums_a_in, sums_a_on, sums_a_far, sums_v, sums_v_in, sums_v_on, sums_v_far, factors_a,
    part_o, part_s, back_o, back_s, mine_o, mine_s,
    vqg, vkg, aqg, akg, pairs,
    load_sem, sa_send, sa_recv, sa_far_send, sa_far_recv, sv_send, sv_recv, sv_far_send, sv_far_recv, fa_send, fa_recv,
    aq_send, aq_recv, ak_send, ak_recv, av_send, av_recv,
    po_send, po_recv, ps_send, ps_recv,
):
    me = lax.axis_index("video")
    mine_z = lax.axis_index("audio")
    side = 2 * lax.rem(me, 2) - 1
    width = vq.shape[1] * n_audio
    heads = vq.shape[1] // E
    v_blocks = vq.shape[0] // BLOCK

    def at(place):
        return lax.rem(me + PLACES[place] * side + n_video, n_video)

    def near(place):
        return (at(place), mine_z)

    def peer(step):
        return (me, lax.rem(mine_z + step + n_audio, n_audio))

    loads = [
        pltpu.make_async_copy(source, target, load_sem.at[i])
        for i, (source, target) in enumerate(
            (
                (aq_hbm, aq.at[0]), (ak_hbm, ak.at[0]), (vk_hbm, vk), (vq_hbm, vq), (pairs_hbm, pairs), (aqg_hbm, aqg),
                (akg_hbm, akg), (vqg_hbm, vqg), (vkg_hbm, vkg), (vv_hbm, vv), (av_hbm, av.at[0]),
            )
        )
    ]
    loads[0].start()
    loads[1].start()
    barrier = pltpu.get_barrier_semaphore()
    for place in range(1, WINDOW):
        pl.semaphore_signal(barrier, inc=1, device_id=near(place), device_id_type=MESH)
    for step in STEPS:
        pl.semaphore_signal(barrier, inc=1, device_id=peer(step), device_id_type=MESH)
    for load in loads[2:]:
        load.start()

    lane = lax.broadcasted_iota(jnp.int32, (BLOCK, 128), 1)

    def row_sums(rows):
        wide = rows.astype(F32)
        return jnp.sum(wide * wide, axis=1, keepdims=True)

    loads[0].wait()
    loads[1].wait()
    table = jnp.where(lane == 0, row_sums(aq[0]), 0.0)
    table = jnp.where(lane == 1, row_sums(ak[0]), table)
    sums_a[...] = table.T[:2]

    pl.semaphore_wait(barrier, WINDOW - 1 + len(STEPS))

    sent = []

    def push(source, into, slot, send, recv, place):
        copy = pltpu.make_async_remote_copy(
            src_ref=source, dst_ref=into.at[slot], send_sem=send, recv_sem=recv.at[slot],
            device_id=near(place), device_id_type=MESH,
        )
        copy.start()
        sent.append(copy)

    def exchange(source, into, send, recv):
        copies = [
            pltpu.make_async_remote_copy(
                src_ref=source, dst_ref=into.at[STEPS.index(-step)], send_sem=send.at[i], recv_sem=recv.at[STEPS.index(-step)],
                device_id=peer(step), device_id_type=MESH,
            )
            for i, step in enumerate(STEPS)
        ]
        for copy in copies:
            copy.start()
        sent.extend(copies)
        return copies

    def pass_on(arrivals, copies, on, far, send, recv):
        for copy in copies:
            copy.wait_recv()
        on[...] = arrivals[STEPS.index(1)] + arrivals[STEPS.index(2)]
        copies = [
            pltpu.make_async_remote_copy(
                src_ref=source, dst_ref=far.at[i], send_sem=send.at[i], recv_sem=recv.at[i],
                device_id=peer(step), device_id_type=MESH,
            )
            for i, (source, step) in enumerate(((on, -2), (arrivals.at[STEPS.index(-1)], 2)))
        ]
        for copy in copies:
            copy.start()
        sent.extend(copies)
        return copies

    def factors(own, arrivals, far, copies):
        total = own[...]
        for i in range(len(STEPS)):
            total = total + arrivals[i]
        for i, copy in enumerate(copies):
            copy.wait_recv()
            total = total + far[i]
        return lax.rsqrt(total / width + EPS)

    def spread(source, into, send, recv):
        for i, place in enumerate((AHEAD, BEHIND, OTHER)):
            push(source, into, MIRROR[place], send.at[i], recv, place)

    def arrived(ref, recv, slot):
        pltpu.make_async_remote_copy(
            src_ref=ref.at[slot], dst_ref=ref.at[slot], send_sem=recv.at[slot], recv_sem=recv.at[slot],
            device_id=near(OTHER), device_id_type=MESH,
        ).wait_recv()

    def relay(ref, send, recv):
        arrived(ref, recv, BEHIND)
        push(ref.at[BEHIND], ref, BESIDE, send.at[3], recv, OTHER)

    sa_copies = exchange(sums_a, sums_a_in, sa_send, sa_recv)
    spread(aq_hbm, aq, aq_send, aq_recv)
    spread(ak_hbm, ak, ak_send, ak_recv)
    spread(av_hbm, av, av_send, av_recv)

    loads[2].wait()
    loads[3].wait()
    table = jnp.zeros((BLOCK, 128), F32)
    for block in range(v_blocks):
        rows = slice(block * BLOCK, (block + 1) * BLOCK)
        table = jnp.where(lane == block, row_sums(vk[rows, :]), table)
        table = jnp.where(lane == v_blocks + block, row_sums(vq[rows, :]), table)
    sums_v[...] = table.T[: 2 * v_blocks]
    sv_copies = exchange(sums_v, sums_v_in, sv_send, sv_recv)

    for load in loads[4:]:
        load.wait()
    row_id = lax.broadcasted_iota(jnp.int32, (v_blocks, 128), 0) + me * v_blocks
    lane_id = lax.broadcasted_iota(jnp.int32, (v_blocks, 128), 1)
    low = jnp.full((v_blocks, 128), MASKED, F32)
    for place in range(WINDOW):
        where = at(place)
        for k in range(pairs.shape[0]):
            low = jnp.where((lane_id == place) & (row_id == pairs[k, where]), 0.0, low)
    low = jnp.where(lane_id < WINDOW, low, 0.0)
    for block in range(v_blocks):
        mask[block * BLOCK : (block + 1) * BLOCK, :] = jnp.broadcast_to(low[block : block + 1], (BLOCK, 128)).astype(BF16)

    gain_a = (aqg[...] * vkg[...] * SCORE_SCALE)[None, :]
    gain_v = (vqg[...] * akg[...] * SCORE_SCALE)[None, :]
    vq[...] = (vq[...].astype(F32) * gain_v).astype(BF16)

    def chosen(place):
        return jnp.where(lane == place, 1.0, 0.0).astype(BF16)

    def marked(rows, place):
        return jnp.concatenate([rows, chosen(place)], axis=1)

    def span(places):
        return slice(places[0] * BLOCK, (places[-1] + 1) * BLOCK)

    def audio_scores(places):
        for h in range(heads):
            queries = jnp.concatenate(
                [marked((head(aq.at[place], h).astype(F32) * head(gain_a, h)).astype(BF16), place) for place in places], axis=0
            )
            keys = jnp.concatenate([head(vk, h), mask[...]], axis=1)
            scores_a[h, span(places), :] = contract_last(queries, keys)

    def video_scores(places):
        for h in range(heads):
            keys = jnp.concatenate([marked(head(ak.at[place], h), place) for place in places], axis=0)
            queries = jnp.concatenate([head(vq, h), mask[...]], axis=1)
            scores_v[h, :, span(places)] = contract_last(queries, keys)

    def blend(scores, top, query_scale, values):
        weights = jnp.exp2((scores - top) * query_scale).astype(BF16)
        ones = jnp.ones(values.shape, BF16)
        mixed = jnp.dot(weights, jnp.concatenate([values, ones], axis=1), preferred_element_type=F32)
        return top * query_scale, mixed[:, :E], mixed[:, E:]

    def as_columns(pieces):
        rows = sum(piece.shape[0] for piece in pieces)
        return jnp.concatenate(list(pieces) + [jnp.zeros((128 - rows, 128), F32)], axis=0).T

    sa_copies = pass_on(sums_a_in, sa_copies, sums_a_on, sums_a_far, sa_far_send, sa_far_recv)
    audio_scores((0,))
    video_scores((0,))
    relay(aq, aq_send, aq_recv)
    sv_copies = pass_on(sums_v_in, sv_copies, sums_v_on, sums_v_far, sv_far_send, sv_far_recv)
    factors_a[0] = factors(sums_a, sums_a_in, sums_a_far, sa_copies)
    for place in (AHEAD, BEHIND, BESIDE, OTHER):
        push(factors_a.at[0], factors_a, MIRROR[place], fa_send.at[place - 1], fa_recv, place)

    arrived(aq, aq_recv, AHEAD)
    audio_scores((AHEAD, BEHIND))
    arrived(ak, ak_recv, AHEAD)
    relay(ak, ak_send, ak_recv)
    for place in (OTHER, BESIDE):
        arrived(aq, aq_recv, place)
    audio_scores((OTHER, BESIDE))
    video_scores((AHEAD, BEHIND))

    factors_v = factors(sums_v, sums_v_in, sums_v_far, sv_copies)
    scale_k = jnp.concatenate([factors_v[block : block + 1] for block in range(v_blocks)], axis=1)

    def audio_tops(places):
        tops = []
        for h in range(heads):
            scaled = scores_a[h, span(places), :] * scale_k
            scores_a[h, span(places), :] = scaled
            tops.append(jnp.max(scaled, axis=1, keepdims=True))
        return tops

    def audio_part(places, tops):
        columns = as_columns([factors_a[place] for place in places])
        query_scale = jnp.concatenate([columns[:, 2 * i : 2 * i + 1] for i in range(len(places))], axis=0)
        logs = [jnp.zeros((BLOCK, 128), F32) for _ in places]
        for h in range(heads):
            top, mixed, total = blend(scores_a[h, span(places), :], tops[h], query_scale, head(vv, h))
            result = mixed / total
            log = top + jnp.log2(total)
            for i, place in enumerate(places):
                rows = slice(i * BLOCK, (i + 1) * BLOCK)
                logs[i] = jnp.where(lane == h, log[rows], logs[i])
                if place == 0:
                    mine_o[h] = result[rows]
                else:
                    part_o[place - 1, h] = result[rows].astype(BF16)
        for i, place in enumerate(places):
            if place == 0:
                mine_s[...] = logs[i].T[:8]
            else:
                part_s[place - 1] = logs[i].T[:8]
                push(part_o.at[place - 1], back_o, MIRROR[place], po_send.at[place - 1], po_recv, place)
                push(part_s.at[place - 1], back_s, MIRROR[place], ps_send.at[place - 1], ps_recv, place)

    audio_part((0,), audio_tops((0,)))
    tops_far = audio_tops((AHEAD, BEHIND))
    tops_near = audio_tops((OTHER, BESIDE))
    relay(av, av_send, av_recv)
    arrived(factors_a, fa_recv, AHEAD)
    arrived(factors_a, fa_recv, BEHIND)
    audio_part((AHEAD, BEHIND), tops_far)
    arrived(factors_a, fa_recv, OTHER)
    arrived(factors_a, fa_recv, BESIDE)
    audio_part((OTHER, BESIDE), tops_near)

    for place in (OTHER, BESIDE):
        arrived(ak, ak_recv, place)
    video_scores((OTHER, BESIDE))
    for place in (OTHER, AHEAD, BESIDE):
        arrived(av, av_recv, place)
    scale_a = jnp.concatenate([factors_a[place, 1:2] for place in range(WINDOW)], axis=1)
    columns_v = as_columns([factors_v[v_blocks:]])
    query_scale = jnp.concatenate([columns_v[:, block : block + 1] for block in range(v_blocks)], axis=0)
    for h in range(heads):
        values = jnp.concatenate([head(av.at[place], h) for place in range(WINDOW)], axis=0)
        for part in range(PARTS):
            rows = slice(part * vq.shape[0] // PARTS, (part + 1) * vq.shape[0] // PARTS)
            scaled = scores_v[h, rows, :] * scale_a
            _, mixed, total = blend(scaled, jnp.max(scaled, axis=1, keepdims=True), query_scale[rows], values)
            vout[rows, h * E : (h + 1) * E] = mixed / total

    for place in range(1, WINDOW):
        arrived(back_s, ps_recv, place)
        arrived(back_o, po_recv, place)
    logs = as_columns([mine_s[...]] + [back_s[place] for place in range(1, WINDOW)])
    for h in range(heads):
        cols = [logs[:, 8 * i + h : 8 * i + h + 1] for i in range(WINDOW)]
        top = cols[0]
        for col in cols[1:]:
            top = jnp.maximum(top, col)
        scales = [jnp.exp2(col - top) for col in cols]
        total = scales[0]
        for scale in scales[1:]:
            total = total + scale
        mixed = scales[0] * mine_o[h]
        for place in range(1, WINDOW):
            mixed = mixed + scales[place] * back_o[place, h].astype(F32)
        aout[:, h * E : (h + 1) * E] = mixed / total

    for copy in sent:
        copy.wait_send()


def solution(mesh):
    n_video, n_audio = mesh.shape["video"], mesh.shape["audio"]

    def body(vq, vk, vv, aq, ak, av, vqg, vkg, aqg, akg, pairs):
        rows_v, wide = vq.shape
        rows_a = aq.shape[0]
        blocks = rows_v // BLOCK
        heads = wide // E
        in_hbm = pl.BlockSpec(memory_space=pltpu.HBM)
        in_vmem = pl.BlockSpec(memory_space=pltpu.VMEM)
        dma = pltpu.SemaphoreType.DMA
        near = WINDOW - 1
        return pl.pallas_call(
            lambda *refs: kernel(n_video, n_audio, *refs),
            out_shape=(pltpu.VMEM((rows_v, wide), F32), pltpu.VMEM((rows_a, wide), F32)),
            in_specs=[in_hbm] * 11,
            out_specs=(in_vmem, in_vmem),
            scratch_shapes=[
                pltpu.VMEM((rows_v, wide), BF16),
                pltpu.VMEM((rows_v, wide), BF16),
                pltpu.VMEM((rows_v, wide), BF16),
                pltpu.VMEM((WINDOW, rows_a, wide), BF16),
                pltpu.VMEM((WINDOW, rows_a, wide), BF16),
                pltpu.VMEM((WINDOW, rows_a, wide), BF16),
                pltpu.VMEM((rows_v, 128), BF16),
                pltpu.VMEM((heads, WINDOW * rows_a, rows_v), F32),
                pltpu.VMEM((heads, rows_v, WINDOW * rows_a), F32),
                pltpu.VMEM((2, 128), F32),
                pltpu.VMEM((len(STEPS), 2, 128), F32),
                pltpu.VMEM((2, 128), F32),
                pltpu.VMEM((2, 2, 128), F32),
                pltpu.VMEM((2 * blocks, 128), F32),
                pltpu.VMEM((len(STEPS), 2 * blocks, 128), F32),
                pltpu.VMEM((2 * blocks, 128), F32),
                pltpu.VMEM((2, 2 * blocks, 128), F32),
                pltpu.VMEM((WINDOW, 2, 128), F32),
                pltpu.VMEM((near, heads, rows_a, E), BF16),
                pltpu.VMEM((near, 8, 128), F32),
                pltpu.VMEM((WINDOW, heads, rows_a, E), BF16),
                pltpu.VMEM((WINDOW, 8, 128), F32),
                pltpu.VMEM((heads, rows_a, E), F32),
                pltpu.VMEM((8, 128), F32),
                pltpu.VMEM((wide,), F32),
                pltpu.VMEM((wide,), F32),
                pltpu.VMEM((wide,), F32),
                pltpu.VMEM((wide,), F32),
                pltpu.SMEM(pairs.shape[::-1], jnp.int32),
                dma((11,)),
                dma((len(STEPS),)),
                dma((len(STEPS),)),
                dma((2,)),
                dma((2,)),
                dma((len(STEPS),)),
                dma((len(STEPS),)),
                dma((2,)),
                dma((2,)),
                dma((near,)),
                dma((WINDOW,)),
                dma((near,)),
                dma((WINDOW,)),
                dma((near,)),
                dma((WINDOW,)),
                dma((near,)),
                dma((WINDOW,)),
                dma((near,)),
                dma((WINDOW,)),
                dma((near,)),
                dma((WINDOW,)),
            ],
            compiler_params=pltpu.CompilerParams(
                collective_id=0, has_side_effects=True, vmem_limit_bytes=VMEM_LIMIT
            ),
            name="paired_attention",
        )(vq, vk, vv, aq, ak, av, vqg, vkg, aqg, akg, pairs.T)

    both = P("video", "audio")
    return jax.shard_map(
        body,
        mesh=mesh,
        in_specs=(both,) * 6 + (P("audio"),) * 4 + (P(),),
        out_specs=(both, both),
        check_vma=False,
    )
```
